128 devices in a mesh: clip: 4 (over z_hi, core), tm: 32 (over x, z_lo, y).
Axes of the slice: x: 4, y: 4, z: 4 (z_hi: 2, z_lo: 2; z = z_hi * 2 + z_lo), core: 2. Of those that a mesh axis runs over, the one named last changes fastest.
Arguments:
- clips: bfloat16 [16, 32, 128, 1024], P('clip', 'tm'), may hold values from -6 to 6
- w_qkv: bfloat16 [1024, 3072], replicated, may hold values from -8 to 8
- w_out: bfloat16 [1024, 1024], replicated, may hold values from -0.1875 to 0.1875
- cotangent: bfloat16 [16, 32, 128, 1024], P('clip', 'tm'), may hold values from -6 to 6
Outputs:
- grad_clips: bfloat16 [16, 32, 128, 1024], P('clip', 'tm')
- grad_qkv: float32 [1024, 3072], P(('clip', 'tm'))
- grad_out: float32 [1024, 1024], P(('clip', 'tm'))
The draws below stay inside these ranges and needn't reach their ends.
All inputs are finite; a program needn't handle non-finite values.
Results may differ from the reference program's by a relative error of at most 0.0093.
Values may be sent and summed in bfloat16 or wider, within the bound.
A program may use at most 128 MiB of HBM per device.

```python
import jax
import jax.numpy as jnp
from jax import lax

D = 1024
HEADS = 16
PATCH = 128
CLIPS = 16
FRAMES = 32


def draw_w_qkv(key, part):
    key = jax.random.fold_in(key, 11)
    first = jax.random.fold_in(key, 0)
    base = jax.random.normal(first, (D, 3 * D), jnp.float32) * D ** (-0.5)
    return jnp.clip(base, -8.0, 8.0).astype(jnp.bfloat16)


def strengthened(values, stream_key, source, target, parts, factor):
    def block_of(dim):
        return (jnp.arange(values.shape[dim]) // (values.shape[dim] // parts)).reshape((-1,) + (1,) * (values.ndim - 1 - dim))

    first = jax.random.permutation(stream_key, parts)[block_of(target)]
    other_side = (block_of(target) + parts // 2) % parts
    return jnp.where((block_of(source) == first) | (block_of(source) == other_side), factor * values, values)


def block_scale(rng, dims, shards, smallest, largest):
    def one(position, blocks):
        draws = jax.random.uniform(jax.random.fold_in(jax.random.fold_in(rng, 6), position), (blocks,), jnp.float32, smallest / len(shards), largest / len(shards))
        return jnp.repeat(jnp.exp(draws), dims[position] // blocks).reshape((-1,) + (1,) * (len(dims) - position - 1))

    loudness = one(*shards[0])
    for cut in shards[1:]:
        loudness = loudness * one(*cut)
    return loudness


def gaussian(stream_key, extent, deviation, limit, cuts=(), dtype=jnp.bfloat16):
    entries = deviation * jax.random.normal(stream_key, extent, jnp.float32)
    if cuts:
        entries = entries * block_scale(stream_key, extent, cuts, -0.22, 0.18)
    return jnp.clip(entries, -limit, limit).astype(dtype)


def heavy_noise(rng, shape, deviation, limit, cuts, heavy, kind=jnp.bfloat16):
    values = deviation * jax.random.normal(rng, shape, jnp.float32)
    if cuts:
        values = values * block_scale(rng, shape, cuts, -0.22, 0.18)
    return jnp.clip(strengthened(values, jax.random.fold_in(rng, 3), *heavy), -limit, limit).astype(kind)


def setup_inputs(seed: int = 0) -> dict:
    key_of = jax.random.split(jax.random.key(seed), 5)
    clips = heavy_noise(key_of[0], (CLIPS, FRAMES, PATCH, D), 1.0, 6.0, ((0, 4), (1, 32)), (1, 3, 32, 2.75))
    w_qkv = draw_w_qkv(jax.random.fold_in(key_of[4], 71), 0)
    w_out = gaussian(key_of[2], (D, D), D ** -0.5, 0.1875)
    cotangent = gaussian(key_of[3], (CLIPS, FRAMES, PATCH, D), 1.0, 6.0, ((0, 4), (1, 32)))
    return dict(clips=clips, w_qkv=w_qkv, w_out=w_out, cotangent=cotangent)


epsilon = 1e-06

def normalize(clips):
    values32 = clips.astype(jnp.float32)
    centred = values32 - lax.optimization_barrier(jnp.mean(values32, axis=-1, keepdims=True))
    inverse = lax.rsqrt(lax.optimization_barrier(jnp.mean(centred * centred, axis=-1, keepdims=True)) + epsilon)
    return (centred * inverse, inverse)

def split_heads(array):
    return array.reshape(array.shape[:-1] + (HEADS, array.shape[-1] // HEADS))

def unpack(packed):
    width = packed.shape[-1] // 3
    queries = split_heads(packed[..., :width]).astype(jnp.float32)
    key_rows = split_heads(packed[..., width:2 * width]).astype(jnp.float32)
    value_rows = split_heads(packed[..., 2 * width:]).astype(jnp.float32)
    return (queries, key_rows, value_rows, width)

def attend(packed):
    queries, key_rows, value_rows, width = unpack(packed)
    scaling = (width // HEADS) ** (-0.5)
    scores = jnp.einsum('cfphd,cgphd->cphfg', queries, key_rows) * scaling
    highest = lax.optimization_barrier(jnp.max(scores, axis=-1, keepdims=True))
    expo = jnp.exp(scores - highest)
    full_weights = expo / lax.optimization_barrier(jnp.sum(expo, axis=-1, keepdims=True))
    low_weights = full_weights.astype(jnp.bfloat16)
    mixed = jnp.einsum('cphfg,cgphd->cfphd', low_weights.astype(jnp.float32), value_rows)
    mixed = mixed.astype(jnp.bfloat16).reshape(packed.shape[:3] + (width,))
    return (mixed, full_weights, low_weights)

def attend_back(packed, full_weights, low_weights, mixed_grad):
    queries, key_rows, value_rows, width = unpack(packed)
    scaling = (width // HEADS) ** (-0.5)
    grad_heads = split_heads(mixed_grad).astype(jnp.float32)
    dots = jnp.einsum('cfphd,cgphd->cphfg', grad_heads, value_rows)
    score_grad = full_weights * (dots - lax.optimization_barrier(jnp.sum(full_weights * dots, axis=-1, keepdims=True)))
    score_grad = (score_grad * scaling).astype(jnp.bfloat16).astype(jnp.float32)
    query_grad = jnp.einsum('cphfg,cgphd->cfphd', score_grad, key_rows).astype(jnp.bfloat16)
    key_grad = jnp.einsum('cphfg,cfphd->cgphd', score_grad, queries).astype(jnp.bfloat16)
    value_grad = jnp.einsum('cphfg,cfphd->cgphd', low_weights.astype(jnp.float32), grad_heads).astype(jnp.bfloat16)
    lead = packed.shape[:3] + (width,)
    return jnp.concatenate([query_grad.reshape(lead), key_grad.reshape(lead), value_grad.reshape(lead)], axis=-1)

def reference(clips, w_qkv, w_out, cotangent):
    unit_rows, inverse = normalize(clips)
    normed = unit_rows.astype(jnp.bfloat16)
    flat_normed = normed.reshape(-1, D)
    packed = jnp.dot(flat_normed, w_qkv, preferred_element_type=jnp.float32).astype(jnp.bfloat16)
    packed = packed.reshape(clips.shape[:3] + (3 * D,))
    mixed, full_weights, low_weights = attend(packed)
    flat_cot = cotangent.reshape(-1, D)
    grad_out = jnp.dot(mixed.reshape(-1, D).T, flat_cot, preferred_element_type=jnp.float32)
    mixed_grad = jnp.dot(flat_cot, w_out.T, preferred_element_type=jnp.float32).astype(jnp.bfloat16)
    packed_grad = attend_back(packed, full_weights, low_weights, mixed_grad.reshape(mixed.shape))
    flat_grad = packed_grad.reshape(-1, 3 * D)
    grad_qkv = jnp.dot(flat_normed.T, flat_grad, preferred_element_type=jnp.float32)
    normed_grad = jnp.dot(flat_grad, w_qkv.T, preferred_element_type=jnp.float32).reshape(clips.shape)
    input_grad = inverse * (normed_grad - lax.optimization_barrier(jnp.mean(normed_grad, axis=-1, keepdims=True)) - unit_rows * lax.optimization_barrier(jnp.mean(normed_grad * unit_rows, axis=-1, keepdims=True)))
    grad_clips = (cotangent.astype(jnp.float32) + input_grad).astype(jnp.bfloat16)
    return (grad_clips, grad_qkv, grad_out)
```

```python
import jax
import jax.numpy as jnp
from jax import lax
from jax.sharding import PartitionSpec as P

D = 1024
HEADS = 16
EPSILON = 1e-06


def normalize(rows):
    values32 = rows.astype(jnp.float32)
    centred = values32 - jnp.mean(values32, axis=-1, keepdims=True)
    inverse = lax.rsqrt(jnp.mean(centred * centred, axis=-1, keepdims=True) + EPSILON)
    return centred * inverse, inverse


def heads_of(array, frames, patches):
    return array.reshape(frames, patches, HEADS, D // HEADS)


def attention(packed, mixed_grad, frames, patches):
    queries, keys, values = (heads_of(packed[:, i * D : (i + 1) * D], frames, patches) for i in range(3))
    grads = heads_of(mixed_grad, frames, patches)
    scaling = (D // HEADS) ** (-0.5)
    f32 = jnp.float32
    scores = jnp.einsum("fphd,gphd->phfg", queries, keys, preferred_element_type=f32) * scaling
    expo = jnp.exp(scores - jnp.max(scores, axis=-1, keepdims=True))
    full = expo / jnp.sum(expo, axis=-1, keepdims=True)
    low = full.astype(jnp.bfloat16)
    mixed = jnp.einsum("phfg,gphd->fphd", low, values, preferred_element_type=f32)
    dots = jnp.einsum("fphd,gphd->phfg", grads, values, preferred_element_type=f32)
    score_grad = full * (dots - jnp.sum(full * dots, axis=-1, keepdims=True))
    score_grad = (score_grad * scaling).astype(jnp.bfloat16)
    query_grad = jnp.einsum("phfg,gphd->fphd", score_grad, keys, preferred_element_type=f32)
    key_grad = jnp.einsum("phfg,fphd->gphd", score_grad, queries, preferred_element_type=f32)
    value_grad = jnp.einsum("phfg,fphd->gphd", low, grads, preferred_element_type=f32)
    flat = lambda a: a.astype(jnp.bfloat16).reshape(frames * patches, D)
    return flat(mixed), jnp.concatenate([flat(query_grad), flat(key_grad), flat(value_grad)], axis=-1)


def row_product(left, right):
    return lax.dot_general(left, right, (((0,), (0,)), ((), ())), preferred_element_type=jnp.float32)


def scatter_sum(partial, axes):
    total = partial
    for axis in axes:
        n = lax.axis_size(axis)
        blocks = total.astype(jnp.bfloat16).reshape(n, -1, partial.shape[-1])
        got = lax.all_to_all(blocks, axis, split_axis=0, concat_axis=0, tiled=True)
        total = jnp.sum(got.astype(jnp.float32), axis=0)
    return total


def shards(clips, w_qkv, w_out, cotangent):
    frames = lax.axis_size("tm")
    patches = clips.shape[0] * clips.shape[1] * clips.shape[2] // frames

    def to_positions(array):
        blocks = array.reshape(frames, patches, D)
        return lax.all_to_all(blocks, "tm", split_axis=0, concat_axis=0, tiled=True).reshape(-1, D)

    rows = to_positions(clips)
    cot = to_positions(cotangent)
    unit_rows, inverse = normalize(rows)
    normed = unit_rows.astype(jnp.bfloat16)
    packed = jnp.dot(normed, w_qkv, preferred_element_type=jnp.float32).astype(jnp.bfloat16)
    mixed_grad = jnp.dot(cot, w_out.T, preferred_element_type=jnp.float32).astype(jnp.bfloat16)
    mixed, packed_grad = attention(packed, mixed_grad, frames, patches)
    partial = jnp.concatenate([row_product(normed, packed_grad), row_product(mixed, cot)], axis=-1)
    total = scatter_sum(partial, ("clip", "tm"))
    normed_grad = lax.dot_general(packed_grad, w_qkv, (((1,), (1,)), ((), ())), preferred_element_type=jnp.float32)
    input_grad = inverse * (
        normed_grad
        - jnp.mean(normed_grad, axis=-1, keepdims=True)
        - unit_rows * jnp.mean(normed_grad * unit_rows, axis=-1, keepdims=True)
    )
    grad = (cot.astype(jnp.float32) + input_grad).astype(jnp.bfloat16)
    grad = lax.all_to_all(grad.reshape(frames, patches, D), "tm", split_axis=0, concat_axis=0, tiled=True)
    return grad.reshape(clips.shape), total[:, : 3 * D], total[:, 3 * D :]


def solution(mesh):
    return jax.shard_map(
        shards,
        mesh=mesh,
        in_specs=(P("clip", "tm", None, None), P(), P(), P("clip", "tm", None, None)),
        out_specs=(P("clip", "tm", None, None), P(("clip", "tm"), None), P(("clip", "tm"), None)),
        check_vma=False,
    )
```

```python
import jax
import jax.numpy as jnp
from jax import lax
from jax.experimental import pallas as pl
from jax.experimental.pallas import tpu as pltpu
from jax.sharding import PartitionSpec as P

D = 1024
WIDTH = 64
PAIRS = 8
FRAMES = 32
PATCHES = 16
ROWS = FRAMES * PATCHES
GROUP = 128
GROUPS = ROWS // GROUP
EPSILON = 1e-06
SCALING = WIDTH ** (-0.5)
NEGATIVE = -1e30
F32 = jnp.float32
BF16 = jnp.bfloat16
MESH = pl.DeviceIdType.MESH
DIGITS = ("x1", "y1", "z1", "x0", "y0", "z0")
CHUNKS = ((0, 1, 2, 3), (4, 5, 6, 7, 8, 9), (10, 11, 12, 13, 14, 15))
STREAMS = 16


def order_of(stream):
    start = stream if stream < 4 else stream - 4
    return tuple(DIGITS[(start + k) % 6] for k in range(6))


def dot(left, right):
    return jnp.dot(left, right, preferred_element_type=F32)


def dot_nt(left, right):
    return lax.dot_general(left, right, (((1,), (1,)), ((), ())), preferred_element_type=F32)


def dot_tn(left, right):
    return lax.dot_general(left, right, (((0,), (0,)), ((), ())), preferred_element_type=F32)


def kernel(
    clips, w_qkv, w_out, cotangent, out, grad_qkv, grad_out,
    clips_in, cot_in, wq, wo, perm, perm_back, unit, inverse, normed, cot, cot_other, packed, weights,
    mixed, mixed_t, mixed_t_other, normed_t, normed_t_other, mixed_grad, back, back_other,
    partial, arrived, grads, leaving, normed_grad,
    local_sem, send_sem, recv_sem, core_send, core_recv, sum_send, sum_recv,
):
    clip, tm = lax.axis_index("clip"), lax.axis_index("tm")
    z_hi, core = clip // 2, clip % 2
    x, z_lo, y = tm // 8, (tm // 4) % 2, tm % 4

    def shifted(k):
        return ((x + k // 8) % 4) * 8 + ((z_lo + (k // 4) % 2) % 2) * 4 + (y + k % 4) % 4

    def tm_of(x, z_lo, y):
        return x * 8 + z_lo * 4 + y

    other_core = {"clip": z_hi * 2 + 1 - core, "tm": tm}
    partner = {
        "x1": {"clip": clip, "tm": tm_of(3 - x, z_lo, y)},
        "x0": {"clip": clip, "tm": tm_of(x + 1 - 2 * (x % 2), z_lo, y)},
        "y1": {"clip": clip, "tm": tm_of(x, z_lo, 3 - y)},
        "y0": {"clip": clip, "tm": tm_of(x, z_lo, y + 1 - 2 * (y % 2))},
        "z1": {"clip": (1 - z_hi) * 2 + core, "tm": tm_of(x, 1 - z_lo, y)},
        "z0": {"clip": clip, "tm": tm_of(x, 1 - z_lo, y)},
    }
    digit = {
        "x1": x // 2, "x0": (x // 2 + x) % 2, "y1": y // 2, "y0": (y // 2 + y) % 2,
        "z1": z_hi, "z0": (z_hi + z_lo) % 2,
    }

    locals_ = [
        pltpu.make_async_copy(w_qkv, wq, local_sem.at[0]),
        pltpu.make_async_copy(w_out, wo, local_sem.at[1]),
        pltpu.make_async_copy(clips.at[tm], clips_in.at[tm], local_sem.at[2]),
        pltpu.make_async_copy(cotangent.at[tm], cot_in.at[tm], local_sem.at[3]),
    ]
    for copy in locals_:
        copy.start()

    barrier = pltpu.get_barrier_semaphore()

    @pl.loop(1, FRAMES)
    def _(k):
        pl.semaphore_signal(barrier, inc=1, device_id={"clip": clip, "tm": shifted(k)}, device_id_type=MESH)

    pl.semaphore_signal(barrier, inc=1, device_id=other_core, device_id_type=MESH)
    pl.semaphore_signal(barrier, inc=1, device_id=partner["z1"], device_id_type=MESH)
    pl.semaphore_wait(barrier, FRAMES + 1)

    def exchange(which, source, target, k):
        there = shifted(k)
        return pltpu.make_async_remote_copy(
            src_ref=source.at[there], dst_ref=target.at[tm],
            send_sem=send_sem.at[which, there], recv_sem=recv_sem.at[which, tm],
            device_id={"clip": clip, "tm": there}, device_id_type=MESH,
        )

    def arrival(which, source, target, k):
        there = shifted(k)
        return pltpu.make_async_remote_copy(
            src_ref=source.at[there], dst_ref=target.at[there],
            send_sem=send_sem.at[which, there], recv_sem=recv_sem.at[which, there],
            device_id={"clip": clip, "tm": there}, device_id_type=MESH,
        )

    def start_all(which, source, target):
        @pl.loop(1, FRAMES)
        def _(k):
            exchange(which, source, target, k).start()

    def wait_all(which, source, target):
        @pl.loop(1, FRAMES)
        def _(k):
            arrival(which, source, target, k).wait_recv()

    def sent_all(which, source, target):
        @pl.loop(1, FRAMES)
        def _(k):
            exchange(which, source, target, k).wait_send()

    def to_core(index, source, target):
        return pltpu.make_async_remote_copy(
            src_ref=source, dst_ref=target, send_sem=core_send.at[index], recv_sem=core_recv.at[index],
            device_id=other_core, device_id_type=MESH,
        )

    normed_copies = [to_core(z, normed_t.at[2 * z + 1 - core], normed_t_other.at[z]) for z in range(2)]
    mixed_copies = [to_core(2 + z, mixed_t.at[2 * z + 1 - core], mixed_t_other.at[z]) for z in range(2)]
    cot_copy = to_core(4, cot, cot_other)
    back_copies = [to_core(5 + h, back.at[h], back_other.at[h]) for h in range(2)]
    core_copies = normed_copies + mixed_copies + [cot_copy] + back_copies

    start_all(0, clips, clips_in)
    start_all(1, cotangent, cot_in)

    row = lax.broadcasted_iota(jnp.int32, (ROWS, ROWS), 0)
    column = lax.broadcasted_iota(jnp.int32, (ROWS, ROWS), 1)
    perm[...] = jnp.where((row & 31) * PATCHES + (row >> 5) == column, 1.0, 0.0).astype(BF16)
    perm_back[...] = jnp.where((column & 31) * PATCHES + (column >> 5) == row, 1.0, 0.0).astype(BF16)
    lane = lax.broadcasted_iota(jnp.int32, (GROUP, GROUP), 1)
    low_half = lane < WIDTH
    low_mask = jnp.where(low_half, 1.0, 0.0).astype(BF16)
    high_mask = jnp.where(low_half, 0.0, 1.0).astype(BF16)
    same = (lax.broadcasted_iota(jnp.int32, (2 * GROUP, GROUP), 0) & (GROUP - 1)) >> 5 == (
        lax.broadcasted_iota(jnp.int32, (2 * GROUP, GROUP), 1) >> 5
    )

    def both(array):
        return jnp.concatenate([array * low_mask, array * high_mask], axis=0)

    def join(array):
        return jnp.where(low_half, array[:GROUP], array[GROUP:]).astype(BF16)

    locals_[2].wait()
    wait_all(0, clips, clips_in)

    @pl.loop(0, 4)
    def _(n):
        columns = pl.ds(pl.multiple_of(n * 256, 256), 256)
        unit[:, columns] = dot(perm[...], clips_in[:, :, columns].reshape(ROWS, 256))

    @pl.loop(0, ROWS // 32)
    def _(r):
        rows = pl.ds(pl.multiple_of(r * 32, 32), 32)
        values = unit[rows, :]
        centred = values - jnp.mean(values, axis=-1, keepdims=True)
        scale = lax.rsqrt(jnp.mean(centred * centred, axis=-1, keepdims=True) + EPSILON)
        result = centred * scale
        unit[rows, :] = result
        normed[rows, :] = result.astype(BF16)
        inverse[rows, :] = jnp.broadcast_to(scale, (32, 128))

    for z in range(4):
        normed_t[z] = normed[:, z * 256 : (z + 1) * 256].T
    for copy in normed_copies:
        copy.start()

    locals_[0].wait()

    @pl.loop(0, 12)
    def _(n):
        columns = pl.ds(pl.multiple_of(n * 256, 256), 256)
        packed[:, columns] = dot(normed[...], wq[:, columns]).astype(BF16)

    @pl.loop(0, GROUPS)
    def _(g):
        rows = pl.ds(pl.multiple_of(g * GROUP, GROUP), GROUP)
        for j in range(PAIRS):
            queries = both(packed[rows, j * 128 : (j + 1) * 128])
            keys = packed[rows, D + j * 128 : D + (j + 1) * 128]
            values = packed[rows, 2 * D + j * 128 : 2 * D + (j + 1) * 128]
            scores = jnp.where(same, dot_nt(queries, keys) * SCALING, NEGATIVE)
            expo = jnp.exp(scores - jnp.max(scores, axis=-1, keepdims=True))
            full = expo / jnp.sum(expo, axis=-1, keepdims=True)
            weights[g, j] = full
            mixed[rows, j * 128 : (j + 1) * 128] = join(dot(full.astype(BF16), values))

    for z in range(4):
        mixed_t[z] = mixed[:, z * 256 : (z + 1) * 256].T
    for copy in mixed_copies:
        copy.start()

    locals_[3].wait()
    wait_all(1, cotangent, cot_in)

    @pl.loop(0, 4)
    def _(n):
        columns = pl.ds(pl.multiple_of(n * 256, 256), 256)
        cot[:, columns] = dot(perm[...], cot_in[:, :, columns].reshape(ROWS, 256)).astype(BF16)

    cot_copy.start()
    locals_[1].wait()

    @pl.loop(0, 4)
    def _(n):
        columns = pl.ds(pl.multiple_of(n * 256, 256), 256)
        mixed_grad[:, columns] = dot_nt(cot[...], wo[columns, :]).astype(BF16)

    def attention_back(half):
        @pl.loop(0, GROUPS)
        def _(g):
            rows = pl.ds(pl.multiple_of(g * GROUP, GROUP), GROUP)
            for local in range(PAIRS // 2):
                j = half * (PAIRS // 2) + local
                queries = both(packed[rows, j * 128 : (j + 1) * 128])
                keys = packed[rows, D + j * 128 : D + (j + 1) * 128]
                values = packed[rows, 2 * D + j * 128 : 2 * D + (j + 1) * 128]
                heads = both(mixed_grad[rows, j * 128 : (j + 1) * 128])
                full = weights[g, j]
                dots = dot_nt(heads, values)
                score = full * (dots - jnp.sum(full * dots, axis=-1, keepdims=True))
                score = (score * SCALING).astype(BF16)
                c = local * 128
                back[half, rows, c : c + 128] = join(dot(score, keys))
                back[half, rows, 512 + c : 640 + c] = dot_tn(score, queries).astype(BF16)
                back[half, rows, 1024 + c : 1152 + c] = dot_tn(full.astype(BF16), heads).astype(BF16)

    def block_index(stream):
        order = order_of(stream)

        def place(names, bits, base):
            total = 0
            for k, name in enumerate(names):
                total = total + ((digit[name] + bits[k]) % 2) * (1 << (base - k))
            return total

        cache = {}

        def index(z_hi_, x_, z_lo_, y_):
            gray = {"x1": x_ >> 1, "x0": (x_ >> 1) ^ (x_ & 1), "y1": y_ >> 1, "y0": (y_ >> 1) ^ (y_ & 1),
                    "z1": z_hi_, "z0": z_hi_ ^ z_lo_}
            bits = tuple(gray[name] for name in order)
            for key, names, base in ((bits[:3] + (0,), order[:3], 5), (bits[3:] + (1,), order[3:], 2)):
                if key not in cache:
                    cache[key] = place(names, key, base)
            return cache[bits[:3] + (0,)] + cache[bits[3:] + (1,)]

        return index

    def product(stream, left, left_other, right, right_other):
        index = block_index(stream)
        for z in range(2):
            total = dot(left[2 * z + core], right) + dot(left_other[z], right_other)
            for n in range(32):
                block = total[n * 8 : n * 8 + 8]
                tile = jnp.concatenate([block[:, :128], block[:, 128:]], axis=0).astype(BF16)
                partial[stream, index(z, n // 8, (n // 4) % 2, n % 4)] = tile

    def sum_copy(stream, step):
        half = 1 << (5 - step)
        return pltpu.make_async_remote_copy(
            src_ref=partial.at[stream, pl.ds(half, half)], dst_ref=arrived.at[stream, pl.ds(half, half)],
            send_sem=sum_send.at[stream, step], recv_sem=sum_recv.at[stream, step],
            device_id=partner[order_of(stream)[step]], device_id_type=MESH,
        )

    def start_sum(chunk):
        for stream in CHUNKS[chunk]:
            sum_copy(stream, 0).start()

    def advance(chunk, step):
        half = 1 << (5 - step)
        for stream in CHUNKS[chunk]:
            sum_copy(stream, step).wait_recv()
            total = partial[stream, :half].astype(F32) + arrived[stream, half : 2 * half].astype(F32)
            if step < 5:
                partial[stream, :half] = total.astype(BF16)
                sum_copy(stream, step + 1).start()
            else:
                c = stream * 256 if chunk == 0 else column_of(stream)
                target = grad_out if chunk == 0 else grad_qkv
                target[:, c : c + 128] = total[0, :8]
                target[:, c + 128 : c + 256] = total[0, 8:]

    def column_of(stream):
        half, n = (stream - 4) // 6, (stream - 4) % 6
        return (n // 2) * D + half * 512 + (n % 2) * 256

    def qkv_products(half):
        back_copies[half].wait_recv()
        for n, stream in enumerate(CHUNKS[1 + half]):
            columns = slice(n * 256, (n + 1) * 256)
            product(stream, normed_t, normed_t_other, back[half, :, columns], back_other[half, :, columns])

    attention_back(0)
    back_copies[0].start()
    for copy in mixed_copies + [cot_copy]:
        copy.wait_recv()
    for stream in CHUNKS[0]:
        columns = slice(stream * 256, (stream + 1) * 256)
        product(stream, mixed_t, mixed_t_other, cot[:, columns], cot_other[:, columns])
    start_sum(0)
    attention_back(1)
    back_copies[1].start()
    advance(0, 0)
    for copy in normed_copies:
        copy.wait_recv()
    qkv_products(0)
    start_sum(1)
    advance(0, 1)

    @pl.loop(0, 4)
    def _(n):
        columns = pl.ds(pl.multiple_of(n * 256, 256), 256)
        total = jnp.zeros((ROWS, 256), F32)
        for half in range(2):
            for part in range(3):
                start = part * D + half * 512
                total += dot_nt(back[half, :, part * 512 : part * 512 + 512], wq[columns, start : start + 512])
        normed_grad[:, columns] = total

    advance(0, 2)
    advance(1, 0)

    @pl.loop(0, ROWS // 32)
    def _(r):
        rows = pl.ds(pl.multiple_of(r * 32, 32), 32)
        gradient = normed_grad[rows, :]
        values = unit[rows, :]
        scale = inverse[rows, :][:, :1]
        gradient = scale * (
            gradient
            - jnp.mean(gradient, axis=-1, keepdims=True)
            - values * jnp.mean(gradient * values, axis=-1, keepdims=True)
        )
        grads[rows, :] = (cot[rows, :].astype(F32) + gradient).astype(BF16)

    @pl.loop(0, 4)
    def _(n):
        columns = pl.ds(pl.multiple_of(n * 256, 256), 256)
        leaving[:, :, columns] = dot(perm_back[...], grads[:, columns]).astype(BF16).reshape(FRAMES, PATCHES, 256)

    own = pltpu.make_async_copy(leaving.at[tm], out.at[tm], local_sem.at[4])
    own.start()
    start_all(2, leaving, out)
    advance(0, 3)
    advance(1, 1)
    qkv_products(1)
    start_sum(2)
    advance(0, 4)
    advance(1, 2)
    advance(2, 0)
    advance(0, 5)
    advance(1, 3)
    advance(2, 1)
    advance(1, 4)
    advance(2, 2)
    advance(1, 5)
    advance(2, 3)
    advance(2, 4)
    advance(2, 5)
    own.wait()
    wait_all(2, leaving, out)
    sent_all(0, clips, clips_in)
    sent_all(1, cotangent, cot_in)
    sent_all(2, leaving, out)
    for copy in core_copies:
        copy.wait_send()
    for stream in range(STREAMS):
        for step in range(6):
            sum_copy(stream, step).wait_send()


def shards(clips, w_qkv, w_out, cotangent):
    any_ = pl.BlockSpec(memory_space=pl.ANY)
    vmem = pl.BlockSpec(memory_space=pltpu.VMEM)
    blocks = (FRAMES, PATCHES, D)
    out, grad_qkv, grad_out = pl.pallas_call(
        kernel,
        out_shape=(
            jax.ShapeDtypeStruct(blocks, BF16),
            jax.ShapeDtypeStruct((8, 3 * D), F32),
            jax.ShapeDtypeStruct((8, D), F32),
        ),
        in_specs=[any_] * 4,
        out_specs=(any_, vmem, vmem),
        scratch_shapes=[
            pltpu.VMEM(blocks, BF16),
            pltpu.VMEM(blocks, BF16),
            pltpu.VMEM((D, 3 * D), BF16),
            pltpu.VMEM((D, D), BF16),
            pltpu.VMEM((ROWS, ROWS), BF16),
            pltpu.VMEM((ROWS, ROWS), BF16),
            pltpu.VMEM((ROWS, D), F32),
            pltpu.VMEM((ROWS, 128), F32),
            pltpu.VMEM((ROWS, D), BF16),
            pltpu.VMEM((ROWS, D), BF16),
            pltpu.VMEM((ROWS, D), BF16),
            pltpu.VMEM((ROWS, 3 * D), BF16),
            pltpu.VMEM((GROUPS, PAIRS, 2 * GROUP, GROUP), F32),
            pltpu.VMEM((ROWS, D), BF16),
            pltpu.VMEM((4, 256, ROWS), BF16),
            pltpu.VMEM((2, 256, ROWS), BF16),
            pltpu.VMEM((4, 256, ROWS), BF16),
            pltpu.VMEM((2, 256, ROWS), BF16),
            pltpu.VMEM((ROWS, D), BF16),
            pltpu.VMEM((2, ROWS, 1536), BF16),
            pltpu.VMEM((2, ROWS, 1536), BF16),
            pltpu.VMEM((STREAMS, 64, 16, 128), BF16),
            pltpu.VMEM((STREAMS, 64, 16, 128), BF16),
            pltpu.VMEM((ROWS, D), BF16),
            pltpu.VMEM(blocks, BF16),
            pltpu.VMEM((ROWS, D), F32),
            pltpu.SemaphoreType.DMA((5,)),
            pltpu.SemaphoreType.DMA((3, FRAMES)),
            pltpu.SemaphoreType.DMA((3, FRAMES)),
            pltpu.SemaphoreType.DMA((7,)),
            pltpu.SemaphoreType.DMA((7,)),
            pltpu.SemaphoreType.DMA((STREAMS, 6)),
            pltpu.SemaphoreType.DMA((STREAMS, 6)),
        ],
        compiler_params=pltpu.CompilerParams(
            collective_id=0, has_side_effects=True, vmem_limit_bytes=60 * 1024 * 1024
        ),
        cost_estimate=pl.CostEstimate(flops=12 * 10**9, bytes_accessed=12 * 2**20, transcendentals=2**20),
    )(clips.reshape(blocks), w_qkv, w_out, cotangent.reshape(blocks))
    return out.reshape(clips.shape), grad_qkv, grad_out


def solution(mesh):
    return jax.shard_map(
        shards,
        mesh=mesh,
        in_specs=(P("clip", "tm", None, None), P(), P(), P("clip", "tm", None, None)),
        out_specs=(P("clip", "tm", None, None), P(("clip", "tm"), None), P(("clip", "tm"), None)),
        check_vma=False,
    )
```

```python
import jax
import jax.numpy as jnp
from jax import lax
from jax.experimental import pallas as pl
from jax.experimental.pallas import tpu as pltpu
from jax.sharding import PartitionSpec as P

D = 1024
WIDTH = 64
PAIRS = 8
FRAMES = 32
PATCHES = 16
ROWS = FRAMES * PATCHES
GROUP = 128
GROUPS = ROWS // GROUP
EPSILON = 1e-06
SCALING = WIDTH ** (-0.5)
NEGATIVE = -1e30
F32 = jnp.float32
BF16 = jnp.bfloat16
MESH = pl.DeviceIdType.MESH
AXES = ("x", "y", "z")
CHUNKS = ((0, 1, 2, 3), (4, 5, 6), (7, 8, 9), (10, 11, 12), (13, 14, 15))
STREAMS = 16
QUARTERS = 4
GATE = 8


def order_of(stream):
    return tuple(AXES[(stream + k) % 3] for k in range(3))


def dot(left, right):
    return jnp.dot(left, right, preferred_element_type=F32)


def dot_nt(left, right):
    return lax.dot_general(left, right, (((1,), (1,)), ((), ())), preferred_element_type=F32)


def dot_tn(left, right):
    return lax.dot_general(left, right, (((0,), (0,)), ((), ())), preferred_element_type=F32)


def kernel(
    clips, w_qkv, w_out, cotangent, out, grad_qkv, grad_out,
    clips_in, cot_in, wq, wo, perm, perm_back, unit, inverse, normed, cot, cot_other, packed, weights,
    mixed_t, mixed_t_other, normed_t, normed_t_other, mixed_grad, back, back_other,
    partial, arrived, grads, leaving, normed_grad,
    local_sem, send_sem, recv_sem, core_send, core_recv, sum_send, sum_recv,
):
    clip, tm = lax.axis_index("clip"), lax.axis_index("tm")
    z_hi, core = clip // 2, clip % 2
    x, z_lo, y = tm // 8, (tm // 4) % 2, tm % 4

    def shifted(k):
        return ((x + k // 8) % 4) * 8 + ((z_lo + (k // 4) % 2) % 2) * 4 + (y + k % 4) % 4

    def tm_of(x, z_lo, y):
        return x * 8 + z_lo * 4 + y

    other_core = {"clip": z_hi * 2 + 1 - core, "tm": tm}
    place = {"x": x, "y": y, "z": z_hi * 2 + z_lo}

    def along(axis, step):
        if axis == "x":
            return {"clip": clip, "tm": tm_of((x + step) % 4, z_lo, y)}
        if axis == "y":
            return {"clip": clip, "tm": tm_of(x, z_lo, (y + step) % 4)}
        there = (place["z"] + step) % 4
        return {"clip": there // 2 * 2 + core, "tm": tm_of(x, there % 2, y)}

    locals_ = [
        pltpu.make_async_copy(w_qkv, wq, local_sem.at[0]),
        pltpu.make_async_copy(w_out, wo, local_sem.at[1]),
        pltpu.make_async_copy(clips.at[tm], clips_in.at[tm], local_sem.at[2]),
        pltpu.make_async_copy(cotangent.at[tm], cot_in.at[tm], local_sem.at[3]),
    ]
    for copy in locals_:
        copy.start()

    barrier = pltpu.get_barrier_semaphore()

    for k in range(1, FRAMES):
        pl.semaphore_signal(barrier, inc=1, device_id={"clip": clip, "tm": shifted(k)}, device_id_type=MESH)

    pl.semaphore_signal(barrier, inc=1, device_id=other_core, device_id_type=MESH)
    for step in range(1, 4):
        pl.semaphore_signal(barrier, inc=1, device_id=along("z", step), device_id_type=MESH)
    pl.semaphore_wait(barrier, FRAMES + 3)

    def exchange(which, source, target, k):
        there = shifted(k)
        return pltpu.make_async_remote_copy(
            src_ref=source.at[there], dst_ref=target.at[tm],
            send_sem=send_sem.at[which, there], recv_sem=recv_sem.at[which, tm],
            device_id={"clip": clip, "tm": there}, device_id_type=MESH,
        )

    def arrival(which, source, target, k):
        there = shifted(k)
        return pltpu.make_async_remote_copy(
            src_ref=source.at[there], dst_ref=target.at[there],
            send_sem=send_sem.at[which, there], recv_sem=recv_sem.at[which, there],
            device_id={"clip": clip, "tm": there}, device_id_type=MESH,
        )

    def start_all(which, source, target):
        @pl.loop(1, FRAMES)
        def _(k):
            exchange(which, source, target, k).start()

    def wait_all(which, source, target, first=1, last=FRAMES):
        @pl.loop(first, last)
        def _(k):
            arrival(which, source, target, k).wait_recv()

    def sent_all(which, source, target):
        @pl.loop(1, FRAMES)
        def _(k):
            exchange(which, source, target, k).wait_send()

    def to_core(index, source, target):
        return pltpu.make_async_remote_copy(
            src_ref=source, dst_ref=target, send_sem=core_send.at[index], recv_sem=core_recv.at[index],
            device_id=other_core, device_id_type=MESH,
        )

    normed_copies = [to_core(z, normed_t.at[2 * z + 1 - core], normed_t_other.at[z]) for z in range(2)]
    mixed_copies = [to_core(2 + z, mixed_t.at[2 * z + 1 - core], mixed_t_other.at[z]) for z in range(2)]
    cot_copy = to_core(4, cot, cot_other)
    back_columns = [[pl.ds(part * D + q * 256, 256) for part in range(3)] for q in range(QUARTERS)]
    back_copies = [
        [to_core(5 + q * 3 + n, back.at[:, columns], back_other.at[:, columns]) for n, columns in enumerate(back_columns[q])]
        for q in range(QUARTERS)
    ]
    core_copies = normed_copies + mixed_copies + [cot_copy] + sum(back_copies, [])

    start_all(0, clips, clips_in)
    row = lax.broadcasted_iota(jnp.int32, (ROWS, ROWS), 0)
    column = lax.broadcasted_iota(jnp.int32, (ROWS, ROWS), 1)
    perm[...] = jnp.where((row & 31) * PATCHES + (row >> 5) == column, 1.0, 0.0).astype(BF16)
    perm_back[...] = jnp.where((column & 31) * PATCHES + (column >> 5) == row, 1.0, 0.0).astype(BF16)
    lane = lax.broadcasted_iota(jnp.int32, (GROUP, GROUP), 1)
    low_half = lane < WIDTH
    same = lax.broadcasted_iota(jnp.int32, (GROUP, 2 * GROUP), 0) >> 5 == (
        lax.broadcasted_iota(jnp.int32, (GROUP, 2 * GROUP), 1) & (GROUP - 1)
    ) >> 5

    def both(array, scale=1.0):
        low_mask = jnp.where(low_half, scale, 0.0).astype(BF16)
        high_mask = jnp.where(low_half, 0.0, scale).astype(BF16)
        return jnp.concatenate([array * low_mask, array * high_mask], axis=0)

    locals_[2].wait()
    wait_all(0, clips, clips_in, 1, GATE)
    start_all(1, cotangent, cot_in)
    wait_all(0, clips, clips_in, GATE)

    unit[...] = dot(perm[...], clips_in[...].reshape(ROWS, D))

    @pl.loop(0, ROWS // 32, unroll=4)
    def _(r):
        rows = pl.ds(pl.multiple_of(r * 32, 32), 32)
        values = unit[rows, :]
        centred = values - jnp.mean(values, axis=-1, keepdims=True)
        scale = lax.rsqrt(jnp.mean(centred * centred, axis=-1, keepdims=True) + EPSILON)
        result = centred * scale
        unit[rows, :] = result
        normed[rows, :] = result.astype(BF16)
        inverse[rows, :] = jnp.broadcast_to(scale, (32, 128))

    for n in range(4):
        normed_t[n] = normed[:, n * 256 : (n + 1) * 256].T
    for copy in normed_copies:
        copy.start()

    locals_[0].wait()

    @pl.loop(0, 3)
    def _(n):
        columns = pl.ds(pl.multiple_of(n * D, D), D)
        packed[:, columns] = dot(normed[...], wq[:, columns]).astype(BF16)

    @pl.loop(0, GROUPS)
    def _(g):
        rows = pl.ds(pl.multiple_of(g * GROUP, GROUP), GROUP)
        for j in range(PAIRS):
            queries = both(packed[rows, j * 128 : (j + 1) * 128], SCALING)
            keys = packed[rows, D + j * 128 : D + (j + 1) * 128]
            values = packed[rows, 2 * D + j * 128 : 2 * D + (j + 1) * 128]
            scores = jnp.where(same, dot_nt(keys, queries), NEGATIVE)
            expo = jnp.exp(scores - jnp.max(scores, axis=0, keepdims=True))
            full = expo * (1.0 / jnp.sum(expo, axis=0, keepdims=True))
            weights[g, j] = full
            result = dot(values.T, full.astype(BF16)).astype(BF16)
            mixed_t[j // 2, (j % 2) * 128 : (j % 2) * 128 + WIDTH, rows] = result[:WIDTH, :GROUP]
            mixed_t[j // 2, (j % 2) * 128 + WIDTH : (j % 2 + 1) * 128, rows] = result[WIDTH:, GROUP:]

    for copy in mixed_copies:
        copy.start()

    locals_[3].wait()
    wait_all(1, cotangent, cot_in)

    cot[...] = dot(perm[...], cot_in[...].reshape(ROWS, D)).astype(BF16)

    cot_copy.start()
    locals_[1].wait()

    mixed_grad[...] = dot_nt(cot[...], wo[...]).astype(BF16)

    def attention_back(quarter):
        @pl.loop(0, GROUPS, unroll=2)
        def _(g):
            rows = pl.ds(pl.multiple_of(g * GROUP, GROUP), GROUP)
            for j in range(quarter * 2, quarter * 2 + 2):
                queries = both(packed[rows, j * 128 : (j + 1) * 128], SCALING)
                keys = packed[rows, D + j * 128 : D + (j + 1) * 128]
                values = packed[rows, 2 * D + j * 128 : 2 * D + (j + 1) * 128]
                heads = both(mixed_grad[rows, j * 128 : (j + 1) * 128])
                full = weights[g, j]
                dots = dot_nt(values, heads)
                score = (full * (dots - jnp.sum(full * dots, axis=0, keepdims=True))).astype(BF16)
                query_grad = dot_tn(score, keys)
                query_grad = jnp.where(low_half, query_grad[:GROUP], query_grad[GROUP:]) * SCALING
                c = j * 128
                back[rows, c : c + 128] = query_grad.astype(BF16)
                back[rows, D + c : D + c + 128] = dot(score, queries).astype(BF16)
                back[rows, 2 * D + c : 2 * D + c + 128] = dot(full.astype(BF16), heads).astype(BF16)

    def product(stream, left, left_other, right, right_other):
        order = order_of(stream)
        offset = [[(n + 4 - place[axis]) % 4 * 4 ** (2 - k) for n in range(4)] for k, axis in enumerate(order)]
        pair = [[first + second for second in offset[1]] for first in offset[0]]
        for half in range(2):
            total = dot(left[2 * half + core], right) + dot(left_other[half], right_other)
            for n in range(32):
                at = {"x": n // 8, "z": half * 2 + (n // 4) % 2, "y": n % 4}
                index = pair[at[order[0]]][at[order[1]]] + offset[2][at[order[2]]]
                block = total[n * 8 : n * 8 + 8]
                tile = jnp.concatenate([block[:, :128], block[:, 128:]], axis=0).astype(BF16)
                partial[stream, index] = tile

    def sum_copy(stream, level, step):
        size = 4 ** (2 - level)
        return pltpu.make_async_remote_copy(
            src_ref=partial.at[stream, pl.ds(step * size, size)], dst_ref=arrived.at[stream, pl.ds(step * size, size)],
            send_sem=sum_send.at[stream, level], recv_sem=sum_recv.at[stream, level],
            device_id=along(order_of(stream)[level], step), device_id_type=MESH,
        )

    def sum_all(stream, level, semaphore):
        blocks = pl.ds(4 ** (2 - level), 3 * 4 ** (2 - level))
        return pltpu.make_async_copy(partial.at[stream, blocks], arrived.at[stream, blocks], semaphore.at[stream, level])

    def start_sum(chunk, level=0):
        for step in (2, 1, 3):
            for stream in CHUNKS[chunk]:
                sum_copy(stream, level, step).start()

    def advance(chunk, level):
        size = 4 ** (2 - level)
        for stream in CHUNKS[chunk]:
            sum_all(stream, level, sum_recv).wait()
            total = partial[stream, :size].astype(F32)
            for step in range(1, 4):
                total += arrived[stream, step * size : (step + 1) * size].astype(F32)
            if level < 2:
                partial[stream, :size] = total.astype(BF16)
            else:
                c = stream * 256 if chunk == 0 else column_of(stream)
                target = grad_out if chunk == 0 else grad_qkv
                target[:, c : c + 128] = total[0, :8]
                target[:, c + 128 : c + 256] = total[0, 8:]
        if level < 2:
            start_sum(chunk, level + 1)

    def column_of(stream):
        return (stream - 4) % 3 * D + (stream - 4) // 3 * 256

    def qkv_products(quarter):
        for copy in back_copies[quarter]:
            copy.wait_recv()
        for columns, stream in zip(back_columns[quarter], CHUNKS[1 + quarter]):
            product(stream, normed_t, normed_t_other, back[:, columns], back_other[:, columns])
        start_sum(1 + quarter)

    def back_quarter(quarter):
        attention_back(quarter)
        for copy in back_copies[quarter]:
            copy.start()

    for copy in mixed_copies + [cot_copy]:
        copy.wait_recv()
    for stream in CHUNKS[0]:
        columns = slice(stream * 256, (stream + 1) * 256)
        product(stream, mixed_t, mixed_t_other, cot[:, columns], cot_other[:, columns])
    start_sum(0)
    back_quarter(0)
    back_quarter(1)
    for copy in normed_copies:
        copy.wait_recv()
    qkv_products(0)
    advance(0, 0)
    back_quarter(2)
    qkv_products(1)
    advance(0, 1)
    back_quarter(3)
    qkv_products(2)
    advance(1, 0)
    qkv_products(3)
    advance(0, 2)
    advance(2, 0)
    normed_grad[:256, :] = dot_nt(back[:256, :], wq[...])
    advance(1, 1)
    normed_grad[256:, :] = dot_nt(back[256:, :], wq[...])
    advance(3, 0)
    advance(2, 1)

    @pl.loop(0, ROWS // 32, unroll=4)
    def _(r):
        rows = pl.ds(pl.multiple_of(r * 32, 32), 32)
        gradient = normed_grad[rows, :]
        values = unit[rows, :]
        scale = inverse[rows, :][:, :1]
        gradient = scale * (
            gradient
            - jnp.mean(gradient, axis=-1, keepdims=True)
            - values * jnp.mean(gradient * values, axis=-1, keepdims=True)
        )
        grads[rows, :] = (cot[rows, :].astype(F32) + gradient).astype(BF16)

    leaving[...] = dot(perm_back[...], grads[...]).astype(BF16).reshape(FRAMES, PATCHES, D)

    advance(4, 0)
    own = pltpu.make_async_copy(leaving.at[tm], out.at[tm], local_sem.at[4])
    own.start()
    start_all(2, leaving, out)
    advance(3, 1)
    advance(4, 1)
    advance(1, 2)
    advance(2, 2)
    advance(3, 2)
    advance(4, 2)
    own.wait()
    wait_all(2, leaving, out)
    sent_all(0, clips, clips_in)
    sent_all(1, cotangent, cot_in)
    sent_all(2, leaving, out)
    for copy in core_copies:
        copy.wait_send()
    for stream in range(STREAMS):
        for level in range(3):
            sum_all(stream, level, sum_send).wait()


def shards(clips, w_qkv, w_out, cotangent):
    any_ = pl.BlockSpec(memory_space=pl.ANY)
    vmem = pl.BlockSpec(memory_space=pltpu.VMEM)
    blocks = (FRAMES, PATCHES, D)
    out, grad_qkv, grad_out = pl.pallas_call(
        kernel,
        out_shape=(
            jax.ShapeDtypeStruct(blocks, BF16),
            jax.ShapeDtypeStruct((8, 3 * D), F32),
            jax.ShapeDtypeStruct((8, D), F32),
        ),
        in_specs=[any_] * 4,
        out_specs=(any_, vmem, vmem),
        scratch_shapes=[
            pltpu.VMEM(blocks, BF16),
            pltpu.VMEM(blocks, BF16),
            pltpu.VMEM((D, 3 * D), BF16),
            pltpu.VMEM((D, D), BF16),
            pltpu.VMEM((ROWS, ROWS), BF16),
            pltpu.VMEM((ROWS, ROWS), BF16),
            pltpu.VMEM((ROWS, D), F32),
            pltpu.VMEM((ROWS, 128), F32),
            pltpu.VMEM((ROWS, D), BF16),
            pltpu.VMEM((ROWS, D), BF16),
            pltpu.VMEM((ROWS, D), BF16),
            pltpu.VMEM((ROWS, 3 * D), BF16),
            pltpu.VMEM((GROUPS, PAIRS, GROUP, 2 * GROUP), F32),
            pltpu.VMEM((4, 256, ROWS), BF16),
            pltpu.VMEM((2, 256, ROWS), BF16),
            pltpu.VMEM((4, 256, ROWS), BF16),
            pltpu.VMEM((2, 256, ROWS), BF16),
            pltpu.VMEM((ROWS, D), BF16),
            pltpu.VMEM((ROWS, 3 * D), BF16),
            pltpu.VMEM((ROWS, 3 * D), BF16),
            pltpu.VMEM((STREAMS, 64, 16, 128), BF16),
            pltpu.VMEM((STREAMS, 64, 16, 128), BF16),
            pltpu.VMEM((ROWS, D), BF16),
            pltpu.VMEM(blocks, BF16),
            pltpu.VMEM((ROWS, D), F32),
            pltpu.SemaphoreType.DMA((5,)),
            pltpu.SemaphoreType.DMA((3, FRAMES)),
            pltpu.SemaphoreType.DMA((3, FRAMES)),
            pltpu.SemaphoreType.DMA((17,)),
            pltpu.SemaphoreType.DMA((17,)),
            pltpu.SemaphoreType.DMA((STREAMS, 3)),
            pltpu.SemaphoreType.DMA((STREAMS, 3)),
        ],
        compiler_params=pltpu.CompilerParams(
            collective_id=0, has_side_effects=True, vmem_limit_bytes=60 * 1024 * 1024
        ),
        cost_estimate=pl.CostEstimate(flops=12 * 10**9, bytes_accessed=12 * 2**20, transcendentals=2**20),
    )(clips.reshape(blocks), w_qkv, w_out, cotangent.reshape(blocks))

    def finish(*refs):
        copies = [pltpu.make_async_copy(refs[i], refs[3 + i], refs[6].at[i]) for i in range(3)]
        for copy in copies:
            copy.start()
        for copy in copies:
            copy.wait()

    out, grad_qkv, grad_out = pl.pallas_call(
        finish,
        out_shape=tuple(jax.ShapeDtypeStruct(a.shape, a.dtype) for a in (out, grad_qkv, grad_out)),
        in_specs=[vmem] * 3,
        out_specs=(any_,) * 3,
        scratch_shapes=[pltpu.SemaphoreType.DMA((3,))],
    )(out, grad_qkv, grad_out)
    return out.reshape(clips.shape), grad_qkv, grad_out


def solution(mesh):
    return jax.shard_map(
        shards,
        mesh=mesh,
        in_specs=(P("clip", "tm", None, None), P(), P(), P("clip", "tm", None, None)),
        out_specs=(P("clip", "tm", None, None), P(("clip", "tm"), None), P(("clip", "tm"), None)),
        check_vma=False,
    )
```

```python
import jax
import jax.numpy as jnp
from jax import lax
from jax.experimental import pallas as pl
from jax.experimental.pallas import tpu as pltpu
from jax.sharding import PartitionSpec as P

D = 1024
WIDTH = 64
PAIRS = 8
FRAMES = 32
PATCHES = 16
ROWS = FRAMES * PATCHES
GROUP = 128
GROUPS = ROWS // GROUP
EPSILON = 1e-06
SCALING = WIDTH ** (-0.5)
NEGATIVE = -1e30
F32 = jnp.float32
BF16 = jnp.bfloat16
MESH = pl.DeviceIdType.MESH
AXES = ("x", "y", "z")
CHUNKS = ((0, 1, 2, 3), (4, 5, 6), (7, 8, 9), (10, 11, 12), (13, 14, 15))
STREAMS = 16
QUARTERS = 4
GATE = 12


def order_of(stream):
    return tuple(AXES[(stream + k) % 3] for k in range(3))


def dot(left, right):
    return jnp.dot(left, right, preferred_element_type=F32)


def dot_nt(left, right):
    return lax.dot_general(left, right, (((1,), (1,)), ((), ())), preferred_element_type=F32)


def dot_tn(left, right):
    return lax.dot_general(left, right, (((0,), (0,)), ((), ())), preferred_element_type=F32)


def kernel(
    clips, w_qkv, w_out, cotangent, out, grad_qkv, grad_out,
    clips_in, cot_in, wq, wo, perm, perm_back, unit, inverse, normed, cot, cot_other, packed, weights,
    mixed_t, mixed_t_other, normed_t, normed_t_other, mixed_grad, back, back_other,
    partial, arrived, grads, leaving, normed_grad,
    local_sem, send_sem, recv_sem, core_send, core_recv, sum_send, sum_recv,
):
    clip, tm = lax.axis_index("clip"), lax.axis_index("tm")
    z_hi, core = clip // 2, clip % 2
    x, z_lo, y = tm // 8, (tm // 4) % 2, tm % 4

    def shifted(k):
        return ((x + k + k // 8) % 4) * 8 + ((z_lo + k // 4 + k) % 2) * 4 + (y + k) % 4

    def tm_of(x, z_lo, y):
        return x * 8 + z_lo * 4 + y

    other_core = {"clip": z_hi * 2 + 1 - core, "tm": tm}
    place = {"x": x, "y": y, "z": z_hi * 2 + z_lo}

    def along(axis, step):
        if axis == "x":
            return {"clip": clip, "tm": tm_of((x + step) % 4, z_lo, y)}
        if axis == "y":
            return {"clip": clip, "tm": tm_of(x, z_lo, (y + step) % 4)}
        there = (place["z"] + step) % 4
        return {"clip": there // 2 * 2 + core, "tm": tm_of(x, there % 2, y)}

    locals_ = [
        pltpu.make_async_copy(w_qkv, wq, local_sem.at[0]),
        pltpu.make_async_copy(w_out, wo, local_sem.at[1]),
        pltpu.make_async_copy(clips.at[tm], clips_in.at[tm], local_sem.at[2]),
        pltpu.make_async_copy(cotangent.at[tm], cot_in.at[tm], local_sem.at[3]),
    ]
    for copy in locals_:
        copy.start()

    barrier = pltpu.get_barrier_semaphore()

    for k in range(1, FRAMES):
        pl.semaphore_signal(barrier, inc=1, device_id={"clip": clip, "tm": shifted(k)}, device_id_type=MESH)

    pl.semaphore_signal(barrier, inc=1, device_id=other_core, device_id_type=MESH)
    for step in range(1, 4):
        pl.semaphore_signal(barrier, inc=1, device_id=along("z", step), device_id_type=MESH)
    pl.semaphore_wait(barrier, FRAMES + 3)

    def exchange(which, source, target, k):
        there = shifted(k)
        return pltpu.make_async_remote_copy(
            src_ref=source.at[there], dst_ref=target.at[tm],
            send_sem=send_sem.at[which, there], recv_sem=recv_sem.at[which, tm],
            device_id={"clip": clip, "tm": there}, device_id_type=MESH,
        )

    def arrival(which, source, target, k):
        there = shifted(k)
        return pltpu.make_async_remote_copy(
            src_ref=source.at[there], dst_ref=target.at[there],
            send_sem=send_sem.at[which, there], recv_sem=recv_sem.at[which, there],
            device_id={"clip": clip, "tm": there}, device_id_type=MESH,
        )

    def start_all(which, source, target):
        @pl.loop(1, FRAMES)
        def _(k):
            exchange(which, source, target, k).start()

    def wait_all(which, source, target, first=1, last=FRAMES):
        @pl.loop(first, last)
        def _(k):
            arrival(which, source, target, k).wait_recv()

    def sent_all(which, source, target):
        @pl.loop(1, FRAMES)
        def _(k):
            exchange(which, source, target, k).wait_send()

    def to_core(index, source, target):
        return pltpu.make_async_remote_copy(
            src_ref=source, dst_ref=target, send_sem=core_send.at[index], recv_sem=core_recv.at[index],
            device_id=other_core, device_id_type=MESH,
        )

    normed_copies = [to_core(z, normed_t.at[2 * z + 1 - core], normed_t_other.at[z]) for z in range(2)]
    mixed_copies = [to_core(2 + z, mixed_t.at[2 * z + 1 - core], mixed_t_other.at[z]) for z in range(2)]
    cot_copy = to_core(4, cot, cot_other)
    back_columns = [[pl.ds(part * D + q * 256, 256) for part in range(3)] for q in range(QUARTERS)]
    back_copies = [
        [to_core(5 + q * 3 + n, back.at[:, columns], back_other.at[:, columns]) for n, columns in enumerate(back_columns[q])]
        for q in range(QUARTERS)
    ]
    core_copies = normed_copies + mixed_copies + [cot_copy] + sum(back_copies, [])

    start_all(0, clips, clips_in)
    row = lax.broadcasted_iota(jnp.int32, (ROWS, ROWS), 0)
    column = lax.broadcasted_iota(jnp.int32, (ROWS, ROWS), 1)
    perm[...] = jnp.where((row & 31) * PATCHES + (row >> 5) == column, 1.0, 0.0).astype(BF16)
    perm_back[...] = jnp.where((column & 31) * PATCHES + (column >> 5) == row, 1.0, 0.0).astype(BF16)
    lane = lax.broadcasted_iota(jnp.int32, (GROUP, GROUP), 1)
    low_half = lane < WIDTH
    same = lax.broadcasted_iota(jnp.int32, (GROUP, 2 * GROUP), 0) >> 5 == (
        lax.broadcasted_iota(jnp.int32, (GROUP, 2 * GROUP), 1) & (GROUP - 1)
    ) >> 5

    def both(array, scale=1.0):
        low_mask = jnp.where(low_half, scale, 0.0).astype(BF16)
        high_mask = jnp.where(low_half, 0.0, scale).astype(BF16)
        return jnp.concatenate([array * low_mask, array * high_mask], axis=0)

    locals_[2].wait()
    wait_all(0, clips, clips_in, 1, GATE)
    start_all(1, cotangent, cot_in)
    wait_all(0, clips, clips_in, GATE)

    unit[...] = dot(perm[...], clips_in[...].reshape(ROWS, D))

    @pl.loop(0, ROWS // 32, unroll=4)
    def _(r):
        rows = pl.ds(pl.multiple_of(r * 32, 32), 32)
        values = unit[rows, :]
        centred = values - jnp.mean(values, axis=-1, keepdims=True)
        scale = lax.rsqrt(jnp.mean(centred * centred, axis=-1, keepdims=True) + EPSILON)
        result = centred * scale
        unit[rows, :] = result
        normed[rows, :] = result.astype(BF16)
        inverse[rows, :] = jnp.broadcast_to(scale, (32, 128))

    for n in range(4):
        normed_t[n] = normed[:, n * 256 : (n + 1) * 256].T
    for copy in normed_copies:
        copy.start()

    locals_[0].wait()

    @pl.loop(0, 3)
    def _(n):
        columns = pl.ds(pl.multiple_of(n * D, D), D)
        packed[:, columns] = dot(normed[...], wq[:, columns]).astype(BF16)

    @pl.loop(0, GROUPS)
    def _(g):
        rows = pl.ds(pl.multiple_of(g * GROUP, GROUP), GROUP)
        for j in range(PAIRS):
            queries = both(packed[rows, j * 128 : (j + 1) * 128], SCALING)
            keys = packed[rows, D + j * 128 : D + (j + 1) * 128]
            values = packed[rows, 2 * D + j * 128 : 2 * D + (j + 1) * 128]
            scores = jnp.where(same, dot_nt(keys, queries), NEGATIVE)
            expo = jnp.exp(scores - jnp.max(scores, axis=0, keepdims=True))
            full = expo * (1.0 / jnp.sum(expo, axis=0, keepdims=True))
            weights[g, j] = full
            result = dot(values.T, full.astype(BF16)).astype(BF16)
            mixed_t[j // 2, (j % 2) * 128 : (j % 2) * 128 + WIDTH, rows] = result[:WIDTH, :GROUP]
            mixed_t[j // 2, (j % 2) * 128 + WIDTH : (j % 2 + 1) * 128, rows] = result[WIDTH:, GROUP:]

    for copy in mixed_copies:
        copy.start()

    locals_[3].wait()
    wait_all(1, cotangent, cot_in)

    cot[...] = dot(perm[...], cot_in[...].reshape(ROWS, D)).astype(BF16)

    cot_copy.start()
    locals_[1].wait()

    mixed_grad[...] = dot_nt(cot[...], wo[...]).astype(BF16)

    def attention_back(quarter):
        @pl.loop(0, GROUPS, unroll=2)
        def _(g):
            rows = pl.ds(pl.multiple_of(g * GROUP, GROUP), GROUP)
            for j in range(quarter * 2, quarter * 2 + 2):
                queries = both(packed[rows, j * 128 : (j + 1) * 128], SCALING)
                keys = packed[rows, D + j * 128 : D + (j + 1) * 128]
                values = packed[rows, 2 * D + j * 128 : 2 * D + (j + 1) * 128]
                heads = both(mixed_grad[rows, j * 128 : (j + 1) * 128])
                full = weights[g, j]
                dots = dot_nt(values, heads)
                score = (full * (dots - jnp.sum(full * dots, axis=0, keepdims=True))).astype(BF16)
                query_grad = dot_tn(score, keys)
                query_grad = jnp.where(low_half, query_grad[:GROUP], query_grad[GROUP:]) * SCALING
                c = j * 128
                back[rows, c : c + 128] = query_grad.astype(BF16)
                back[rows, D + c : D + c + 128] = dot(score, queries).astype(BF16)
                back[rows, 2 * D + c : 2 * D + c + 128] = dot(full.astype(BF16), heads).astype(BF16)

    def product(stream, left, left_other, right, right_other):
        order = order_of(stream)
        offset = [[(n + 4 - place[axis]) % 4 * 4 ** (2 - k) for n in range(4)] for k, axis in enumerate(order)]
        pair = [[first + second for second in offset[1]] for first in offset[0]]
        for half in range(2):
            total = dot(left[2 * half + core], right) + dot(left_other[half], right_other)
            for n in range(32):
                at = {"x": n // 8, "z": half * 2 + (n // 4) % 2, "y": n % 4}
                index = pair[at[order[0]]][at[order[1]]] + offset[2][at[order[2]]]
                block = total[n * 8 : n * 8 + 8]
                tile = jnp.concatenate([block[:, :128], block[:, 128:]], axis=0).astype(BF16)
                partial[stream, index] = tile

    def sum_copy(stream, level, step):
        size = 4 ** (2 - level)
        return pltpu.make_async_remote_copy(
            src_ref=partial.at[stream, pl.ds(step * size, size)], dst_ref=arrived.at[stream, pl.ds(step * size, size)],
            send_sem=sum_send.at[stream, level], recv_sem=sum_recv.at[stream, level],
            device_id=along(order_of(stream)[level], step), device_id_type=MESH,
        )

    def sum_all(stream, level, semaphore):
        blocks = pl.ds(4 ** (2 - level), 3 * 4 ** (2 - level))
        return pltpu.make_async_copy(partial.at[stream, blocks], arrived.at[stream, blocks], semaphore.at[stream, level])

    def start_sum(chunk, level=0):
        for step in (2, 1, 3):
            for stream in CHUNKS[chunk]:
                sum_copy(stream, level, step).start()

    def advance(chunk, level):
        size = 4 ** (2 - level)
        for stream in CHUNKS[chunk]:
            sum_all(stream, level, sum_recv).wait()
            total = partial[stream, :size].astype(F32)
            for step in range(1, 4):
                total += arrived[stream, step * size : (step + 1) * size].astype(F32)
            if level < 2:
                partial[stream, :size] = total.astype(BF16)
            else:
                c = stream * 256 if chunk == 0 else column_of(stream)
                target = grad_out if chunk == 0 else grad_qkv
                target[:, c : c + 128] = total[0, :8]
                target[:, c + 128 : c + 256] = total[0, 8:]
        if level < 2:
            start_sum(chunk, level + 1)

    def column_of(stream):
        return (stream - 4) % 3 * D + (stream - 4) // 3 * 256

    def qkv_products(quarter):
        for copy in back_copies[quarter]:
            copy.wait_recv()
        for columns, stream in zip(back_columns[quarter], CHUNKS[1 + quarter]):
            product(stream, normed_t, normed_t_other, back[:, columns], back_other[:, columns])
        start_sum(1 + quarter)

    def back_quarter(quarter):
        attention_back(quarter)
        for copy in back_copies[quarter]:
            copy.start()

    back_quarter(0)
    for copy in mixed_copies + [cot_copy]:
        copy.wait_recv()
    for stream in CHUNKS[0]:
        columns = slice(stream * 256, (stream + 1) * 256)
        product(stream, mixed_t, mixed_t_other, cot[:, columns], cot_other[:, columns])
    start_sum(0)
    back_quarter(1)
    for copy in normed_copies:
        copy.wait_recv()
    qkv_products(0)
    back_quarter(2)
    advance(0, 0)
    qkv_products(1)
    back_quarter(3)
    advance(0, 1)
    qkv_products(2)
    advance(1, 0)
    normed_grad[:256, :] = dot_nt(back[:256, :], wq[...])
    qkv_products(3)
    advance(0, 2)
    advance(2, 0)
    normed_grad[256:, :] = dot_nt(back[256:, :], wq[...])
    advance(1, 1)
    advance(3, 0)
    @pl.loop(0, ROWS // 32, unroll=4)
    def _(r):
        rows = pl.ds(pl.multiple_of(r * 32, 32), 32)
        gradient = normed_grad[rows, :]
        values = unit[rows, :]
        scale = inverse[rows, :][:, :1]
        gradient = scale * (
            gradient
            - jnp.mean(gradient, axis=-1, keepdims=True)
            - values * jnp.mean(gradient * values, axis=-1, keepdims=True)
        )
        grads[rows, :] = (cot[rows, :].astype(F32) + gradient).astype(BF16)

    leaving[...] = dot(perm_back[...], grads[...]).astype(BF16).reshape(FRAMES, PATCHES, D)

    advance(2, 1)
    advance(4, 0)
    advance(3, 1)
    own = pltpu.make_async_copy(leaving.at[tm], out.at[tm], local_sem.at[4])
    own.start()
    start_all(2, leaving, out)
    advance(1, 2)
    advance(4, 1)
    advance(2, 2)
    advance(3, 2)
    advance(4, 2)
    own.wait()
    wait_all(2, leaving, out)
    sent_all(0, clips, clips_in)
    sent_all(1, cotangent, cot_in)
    sent_all(2, leaving, out)
    for copy in core_copies:
        copy.wait_send()
    for stream in range(STREAMS):
        for level in range(3):
            sum_all(stream, level, sum_send).wait()


def shards(clips, w_qkv, w_out, cotangent):
    any_ = pl.BlockSpec(memory_space=pl.ANY)
    vmem = pl.BlockSpec(memory_space=pltpu.VMEM)
    blocks = (FRAMES, PATCHES, D)
    out, grad_qkv, grad_out = pl.pallas_call(
        kernel,
        out_shape=(
            jax.ShapeDtypeStruct(blocks, BF16),
            jax.ShapeDtypeStruct((8, 3 * D), F32),
            jax.ShapeDtypeStruct((8, D), F32),
        ),
        in_specs=[any_] * 4,
        out_specs=(any_, vmem, vmem),
        scratch_shapes=[
            pltpu.VMEM(blocks, BF16),
            pltpu.VMEM(blocks, BF16),
            pltpu.VMEM((D, 3 * D), BF16),
            pltpu.VMEM((D, D), BF16),
            pltpu.VMEM((ROWS, ROWS), BF16),
            pltpu.VMEM((ROWS, ROWS), BF16),
            pltpu.VMEM((ROWS, D), F32),
            pltpu.VMEM((ROWS, 128), F32),
            pltpu.VMEM((ROWS, D), BF16),
            pltpu.VMEM((ROWS, D), BF16),
            pltpu.VMEM((ROWS, D), BF16),
            pltpu.VMEM((ROWS, 3 * D), BF16),
            pltpu.VMEM((GROUPS, PAIRS, GROUP, 2 * GROUP), F32),
            pltpu.VMEM((4, 256, ROWS), BF16),
            pltpu.VMEM((2, 256, ROWS), BF16),
            pltpu.VMEM((4, 256, ROWS), BF16),
            pltpu.VMEM((2, 256, ROWS), BF16),
            pltpu.VMEM((ROWS, D), BF16),
            pltpu.VMEM((ROWS, 3 * D), BF16),
            pltpu.VMEM((ROWS, 3 * D), BF16),
            pltpu.VMEM((STREAMS, 64, 16, 128), BF16),
            pltpu.VMEM((STREAMS, 64, 16, 128), BF16),
            pltpu.VMEM((ROWS, D), BF16),
            pltpu.VMEM(blocks, BF16),
            pltpu.VMEM((ROWS, D), F32),
            pltpu.SemaphoreType.DMA((5,)),
            pltpu.SemaphoreType.DMA((3, FRAMES)),
            pltpu.SemaphoreType.DMA((3, FRAMES)),
            pltpu.SemaphoreType.DMA((17,)),
            pltpu.SemaphoreType.DMA((17,)),
            pltpu.SemaphoreType.DMA((STREAMS, 3)),
            pltpu.SemaphoreType.DMA((STREAMS, 3)),
        ],
        compiler_params=pltpu.CompilerParams(
            collective_id=0, has_side_effects=True, vmem_limit_bytes=60 * 1024 * 1024
        ),
        cost_estimate=pl.CostEstimate(flops=12 * 10**9, bytes_accessed=12 * 2**20, transcendentals=2**20),
    )(clips.reshape(blocks), w_qkv, w_out, cotangent.reshape(blocks))

    def finish(*refs):
        copies = [pltpu.make_async_copy(refs[i], refs[3 + i], refs[6].at[i]) for i in range(3)]
        for copy in copies:
            copy.start()
        for copy in copies:
            copy.wait()

    out, grad_qkv, grad_out = pl.pallas_call(
        finish,
        out_shape=tuple(jax.ShapeDtypeStruct(a.shape, a.dtype) for a in (out, grad_qkv, grad_out)),
        in_specs=[vmem] * 3,
        out_specs=(any_,) * 3,
        scratch_shapes=[pltpu.SemaphoreType.DMA((3,))],
    )(out, grad_qkv, grad_out)
    return out.reshape(clips.shape), grad_qkv, grad_out


def solution(mesh):
    return jax.shard_map(
        shards,
        mesh=mesh,
        in_specs=(P("clip", "tm", None, None), P(), P(), P("clip", "tm", None, None)),
        out_specs=(P("clip", "tm", None, None), P(("clip", "tm"), None), P(("clip", "tm"), None)),
        check_vma=False,
    )
```

```python
import jax
import jax.numpy as jnp
from jax import lax
from jax.experimental import pallas as pl
from jax.experimental.pallas import tpu as pltpu
from jax.sharding import PartitionSpec as P

D = 1024
WIDTH = 64
PAIRS = 8
FRAMES = 32
PATCHES = 16
ROWS = FRAMES * PATCHES
GROUP = 128
GROUPS = ROWS // GROUP
EPSILON = 1e-06
SCALING = WIDTH ** (-0.5)
NEGATIVE = -1e30
F32 = jnp.float32
BF16 = jnp.bfloat16
MESH = pl.DeviceIdType.MESH
AXES = ("x", "y", "z")
CHUNKS = ((0, 1, 2, 3), (4, 5, 6), (7, 8, 9), (10, 11, 12), (13, 14, 15))
STREAMS = 16
QUARTERS = 4
GATE = 15


def order_of(stream):
    return tuple(AXES[(stream + k) % 3] for k in range(3))


def dot(left, right):
    return jnp.dot(left, right, preferred_element_type=F32)


def dot_nt(left, right):
    return lax.dot_general(left, right, (((1,), (1,)), ((), ())), preferred_element_type=F32)


def dot_tn(left, right):
    return lax.dot_general(left, right, (((0,), (0,)), ((), ())), preferred_element_type=F32)


def kernel(
    clips, w_qkv, w_out, cotangent, out, grad_qkv, grad_out,
    clips_in, cot_in, wq, wo, perm, perm_back, unit, inverse, normed, cot, cot_other, packed, weights,
    mixed_t, mixed_t_other, normed_t, normed_t_other, mixed_grad, back, back_other,
    partial, arrived, grads, leaving, normed_grad,
    local_sem, send_sem, recv_sem, core_send, core_recv, sum_send, sum_recv,
):
    clip, tm = lax.axis_index("clip"), lax.axis_index("tm")
    z_hi, core = clip // 2, clip % 2
    x, z_lo, y = tm // 8, (tm // 4) % 2, tm % 4

    def shifted(k):
        return ((x + k + k // 8) % 4) * 8 + ((z_lo + k // 4 + k) % 2) * 4 + (y + k) % 4

    def tm_of(x, z_lo, y):
        return x * 8 + z_lo * 4 + y

    other_core = {"clip": z_hi * 2 + 1 - core, "tm": tm}
    place = {"x": x, "y": y, "z": z_hi * 2 + z_lo}

    def along(axis, step):
        if axis == "x":
            return {"clip": clip, "tm": tm_of((x + step) % 4, z_lo, y)}
        if axis == "y":
            return {"clip": clip, "tm": tm_of(x, z_lo, (y + step) % 4)}
        there = (place["z"] + step) % 4
        return {"clip": there // 2 * 2 + core, "tm": tm_of(x, there % 2, y)}

    locals_ = [
        pltpu.make_async_copy(w_qkv, wq, local_sem.at[0]),
        pltpu.make_async_copy(w_out, wo, local_sem.at[1]),
        pltpu.make_async_copy(clips.at[tm], clips_in.at[tm], local_sem.at[2]),
        pltpu.make_async_copy(cotangent.at[tm], cot_in.at[tm], local_sem.at[3]),
    ]
    for copy in locals_:
        copy.start()

    barrier = pltpu.get_barrier_semaphore()

    for k in range(1, FRAMES):
        pl.semaphore_signal(barrier, inc=1, device_id={"clip": clip, "tm": shifted(k)}, device_id_type=MESH)

    pl.semaphore_signal(barrier, inc=1, device_id=other_core, device_id_type=MESH)
    for step in range(1, 4):
        pl.semaphore_signal(barrier, inc=1, device_id=along("z", step), device_id_type=MESH)
    pl.semaphore_wait(barrier, FRAMES + 3)

    def exchange(which, source, target, k):
        there = shifted(k)
        return pltpu.make_async_remote_copy(
            src_ref=source.at[there], dst_ref=target.at[tm],
            send_sem=send_sem.at[which, there], recv_sem=recv_sem.at[which, tm],
            device_id={"clip": clip, "tm": there}, device_id_type=MESH,
        )

    def arrival(which, source, target, k):
        there = shifted(k)
        return pltpu.make_async_remote_copy(
            src_ref=source.at[there], dst_ref=target.at[there],
            send_sem=send_sem.at[which, there], recv_sem=recv_sem.at[which, there],
            device_id={"clip": clip, "tm": there}, device_id_type=MESH,
        )

    def start_all(which, source, target):
        @pl.loop(1, FRAMES)
        def _(k):
            exchange(which, source, target, k).start()

    def wait_all(which, source, target, first=1, last=FRAMES):
        @pl.loop(first, last)
        def _(k):
            arrival(which, source, target, k).wait_recv()

    def sent_all(which, source, target):
        @pl.loop(1, FRAMES)
        def _(k):
            exchange(which, source, target, k).wait_send()

    def to_core(index, source, target):
        return pltpu.make_async_remote_copy(
            src_ref=source, dst_ref=target, send_sem=core_send.at[index], recv_sem=core_recv.at[index],
            device_id=other_core, device_id_type=MESH,
        )

    normed_copies = [to_core(z, normed_t.at[2 * z + 1 - core], normed_t_other.at[z]) for z in range(2)]
    mixed_copies = [to_core(2 + z, mixed_t.at[2 * z + 1 - core], mixed_t_other.at[z]) for z in range(2)]
    cot_copy = to_core(4, cot, cot_other)
    back_columns = [[pl.ds(part * D + q * 256, 256) for part in range(3)] for q in range(QUARTERS)]
    back_copies = [
        [to_core(5 + q * 3 + n, back.at[:, columns], back_other.at[:, columns]) for n, columns in enumerate(back_columns[q])]
        for q in range(QUARTERS)
    ]
    core_copies = normed_copies + mixed_copies + [cot_copy] + sum(back_copies, [])

    start_all(0, clips, clips_in)
    row = lax.broadcasted_iota(jnp.int32, (ROWS, ROWS), 0)
    column = lax.broadcasted_iota(jnp.int32, (ROWS, ROWS), 1)
    perm[...] = jnp.where((row & 31) * PATCHES + (row >> 5) == column, 1.0, 0.0).astype(BF16)
    perm_back[...] = jnp.where((column & 31) * PATCHES + (column >> 5) == row, 1.0, 0.0).astype(BF16)
    lane = lax.broadcasted_iota(jnp.int32, (GROUP, GROUP), 1)
    low_half = lane < WIDTH
    same = lax.broadcasted_iota(jnp.int32, (GROUP, 2 * GROUP), 0) >> 5 == (
        lax.broadcasted_iota(jnp.int32, (GROUP, 2 * GROUP), 1) & (GROUP - 1)
    ) >> 5

    def both(array, scale=1.0):
        low_mask = jnp.where(low_half, scale, 0.0).astype(BF16)
        high_mask = jnp.where(low_half, 0.0, scale).astype(BF16)
        return jnp.concatenate([array * low_mask, array * high_mask], axis=0)

    locals_[2].wait()
    wait_all(0, clips, clips_in, 1, GATE)
    start_all(1, cotangent, cot_in)
    wait_all(0, clips, clips_in, GATE)

    unit[...] = dot(perm[...], clips_in[...].reshape(ROWS, D))

    @pl.loop(0, ROWS // 32, unroll=4)
    def _(r):
        rows = pl.ds(pl.multiple_of(r * 32, 32), 32)
        values = unit[rows, :]
        centred = values - jnp.mean(values, axis=-1, keepdims=True)
        scale = lax.rsqrt(jnp.mean(centred * centred, axis=-1, keepdims=True) + EPSILON)
        result = centred * scale
        unit[rows, :] = result
        normed[rows, :] = result.astype(BF16)
        inverse[rows, :] = jnp.broadcast_to(scale, (32, 128))

    for n in range(4):
        normed_t[n] = normed[:, n * 256 : (n + 1) * 256].T
    for copy in normed_copies:
        copy.start()

    locals_[0].wait()

    @pl.loop(0, 3)
    def _(n):
        columns = pl.ds(pl.multiple_of(n * D, D), D)
        packed[:, columns] = dot(normed[...], wq[:, columns]).astype(BF16)

    @pl.loop(0, GROUPS)
    def _(g):
        rows = pl.ds(pl.multiple_of(g * GROUP, GROUP), GROUP)
        for j in range(PAIRS):
            queries = both(packed[rows, j * 128 : (j + 1) * 128], SCALING)
            keys = packed[rows, D + j * 128 : D + (j + 1) * 128]
            values = packed[rows, 2 * D + j * 128 : 2 * D + (j + 1) * 128]
            scores = jnp.where(same, dot_nt(keys, queries), NEGATIVE)
            expo = jnp.exp(scores - jnp.max(scores, axis=0, keepdims=True))
            full = expo * (1.0 / jnp.sum(expo, axis=0, keepdims=True))
            weights[g, j] = full
            result = dot(values.T, full.astype(BF16)).astype(BF16)
            mixed_t[j // 2, (j % 2) * 128 : (j % 2) * 128 + WIDTH, rows] = result[:WIDTH, :GROUP]
            mixed_t[j // 2, (j % 2) * 128 + WIDTH : (j % 2 + 1) * 128, rows] = result[WIDTH:, GROUP:]

    for copy in mixed_copies:
        copy.start()

    locals_[3].wait()
    wait_all(1, cotangent, cot_in)

    cot[...] = dot(perm[...], cot_in[...].reshape(ROWS, D)).astype(BF16)

    cot_copy.start()
    locals_[1].wait()

    mixed_grad[...] = dot_nt(cot[...], wo[...]).astype(BF16)

    def attention_back(quarter):
        @pl.loop(0, GROUPS, unroll=2)
        def _(g):
            rows = pl.ds(pl.multiple_of(g * GROUP, GROUP), GROUP)
            for j in range(quarter * 2, quarter * 2 + 2):
                queries = both(packed[rows, j * 128 : (j + 1) * 128], SCALING)
                keys = packed[rows, D + j * 128 : D + (j + 1) * 128]
                values = packed[rows, 2 * D + j * 128 : 2 * D + (j + 1) * 128]
                heads = both(mixed_grad[rows, j * 128 : (j + 1) * 128])
                full = weights[g, j]
                dots = dot_nt(values, heads)
                score = (full * (dots - jnp.sum(full * dots, axis=0, keepdims=True))).astype(BF16)
                query_grad = dot_tn(score, keys)
                query_grad = jnp.where(low_half, query_grad[:GROUP], query_grad[GROUP:]) * SCALING
                c = j * 128
                back[rows, c : c + 128] = query_grad.astype(BF16)
                back[rows, D + c : D + c + 128] = dot(score, queries).astype(BF16)
                back[rows, 2 * D + c : 2 * D + c + 128] = dot(full.astype(BF16), heads).astype(BF16)

    def product(stream, left, left_other, right, right_other):
        order = order_of(stream)
        offset = [[(n + 4 - place[axis]) % 4 * 4 ** (2 - k) for n in range(4)] for k, axis in enumerate(order)]
        pair = [[first + second for second in offset[1]] for first in offset[0]]
        for half in range(2):
            total = dot(left[2 * half + core], right) + dot(left_other[half], right_other)
            for n in range(32):
                at = {"x": n // 8, "z": half * 2 + (n // 4) % 2, "y": n % 4}
                index = pair[at[order[0]]][at[order[1]]] + offset[2][at[order[2]]]
                block = total[n * 8 : n * 8 + 8]
                tile = jnp.concatenate([block[:, :128], block[:, 128:]], axis=0).astype(BF16)
                partial[stream, index] = tile

    def sum_copy(stream, level, step):
        size = 4 ** (2 - level)
        return pltpu.make_async_remote_copy(
            src_ref=partial.at[stream, pl.ds(step * size, size)], dst_ref=arrived.at[stream, pl.ds(step * size, size)],
            send_sem=sum_send.at[stream, level], recv_sem=sum_recv.at[stream, level],
            device_id=along(order_of(stream)[level], step), device_id_type=MESH,
        )

    def sum_all(stream, level, semaphore):
        blocks = pl.ds(4 ** (2 - level), 3 * 4 ** (2 - level))
        return pltpu.make_async_copy(partial.at[stream, blocks], arrived.at[stream, blocks], semaphore.at[stream, level])

    def start_sum(chunk, level=0):
        for step in (2, 1, 3):
            for stream in CHUNKS[chunk]:
                sum_copy(stream, level, step).start()

    def advance(chunk, level):
        size = 4 ** (2 - level)
        for stream in CHUNKS[chunk]:
            sum_all(stream, level, sum_recv).wait()
            total = partial[stream, :size].astype(F32)
            for step in range(1, 4):
                total += arrived[stream, step * size : (step + 1) * size].astype(F32)
            if level < 2:
                partial[stream, :size] = total.astype(BF16)
            else:
                c = stream * 256 if chunk == 0 else column_of(stream)
                target = grad_out if chunk == 0 else grad_qkv
                target[:, c : c + 128] = total[0, :8]
                target[:, c + 128 : c + 256] = total[0, 8:]
        if level < 2:
            start_sum(chunk, level + 1)

    def column_of(stream):
        return (stream - 4) % 3 * D + (stream - 4) // 3 * 256

    def qkv_products(quarter):
        for copy in back_copies[quarter]:
            copy.wait_recv()
        for columns, stream in zip(back_columns[quarter], CHUNKS[1 + quarter]):
            product(stream, normed_t, normed_t_other, back[:, columns], back_other[:, columns])
        start_sum(1 + quarter)

    def back_quarter(quarter):
        attention_back(quarter)
        for copy in back_copies[quarter]:
            copy.start()

    back_quarter(0)
    for copy in mixed_copies + [cot_copy]:
        copy.wait_recv()
    for stream in CHUNKS[0]:
        columns = slice(stream * 256, (stream + 1) * 256)
        product(stream, mixed_t, mixed_t_other, cot[:, columns], cot_other[:, columns])
    start_sum(0)
    back_quarter(1)
    for copy in normed_copies:
        copy.wait_recv()
    qkv_products(0)
    back_quarter(2)
    advance(0, 0)
    qkv_products(1)
    back_quarter(3)
    advance(0, 1)
    qkv_products(2)
    advance(1, 0)
    normed_grad[:256, :] = dot_nt(back[:256, :], wq[...])
    qkv_products(3)
    advance(0, 2)
    advance(2, 0)
    normed_grad[256:, :] = dot_nt(back[256:, :], wq[...])
    advance(1, 1)
    advance(3, 0)
    @pl.loop(0, ROWS // 32, unroll=4)
    def _(r):
        rows = pl.ds(pl.multiple_of(r * 32, 32), 32)
        gradient = normed_grad[rows, :]
        values = unit[rows, :]
        scale = inverse[rows, :][:, :1]
        gradient = scale * (
            gradient
            - jnp.mean(gradient, axis=-1, keepdims=True)
            - values * jnp.mean(gradient * values, axis=-1, keepdims=True)
        )
        grads[rows, :] = (cot[rows, :].astype(F32) + gradient).astype(BF16)

    leaving[...] = dot(perm_back[...], grads[...]).astype(BF16).reshape(FRAMES, PATCHES, D)

    advance(2, 1)
    advance(4, 0)
    advance(3, 1)
    own = pltpu.make_async_copy(leaving.at[tm], out.at[tm], local_sem.at[4])
    own.start()
    start_all(2, leaving, out)
    advance(1, 2)
    advance(4, 1)
    advance(2, 2)
    advance(3, 2)
    advance(4, 2)
    own.wait()
    wait_all(2, leaving, out)
    sent_all(0, clips, clips_in)
    sent_all(1, cotangent, cot_in)
    sent_all(2, leaving, out)
    for copy in core_copies:
        copy.wait_send()
    for stream in range(STREAMS):
        for level in range(3):
            sum_all(stream, level, sum_send).wait()


def shards(clips, w_qkv, w_out, cotangent):
    any_ = pl.BlockSpec(memory_space=pl.ANY)
    vmem = pl.BlockSpec(memory_space=pltpu.VMEM)
    blocks = (FRAMES, PATCHES, D)
    out, grad_qkv, grad_out = pl.pallas_call(
        kernel,
        out_shape=(
            jax.ShapeDtypeStruct(blocks, BF16),
            jax.ShapeDtypeStruct((8, 3 * D), F32),
            jax.ShapeDtypeStruct((8, D), F32),
        ),
        in_specs=[any_] * 4,
        out_specs=(any_, vmem, vmem),
        scratch_shapes=[
            pltpu.VMEM(blocks, BF16),
            pltpu.VMEM(blocks, BF16),
            pltpu.VMEM((D, 3 * D), BF16),
            pltpu.VMEM((D, D), BF16),
            pltpu.VMEM((ROWS, ROWS), BF16),
            pltpu.VMEM((ROWS, ROWS), BF16),
            pltpu.VMEM((ROWS, D), F32),
            pltpu.VMEM((ROWS, 128), F32),
            pltpu.VMEM((ROWS, D), BF16),
            pltpu.VMEM((ROWS, D), BF16),
            pltpu.VMEM((ROWS, D), BF16),
            pltpu.VMEM((ROWS, 3 * D), BF16),
            pltpu.VMEM((GROUPS, PAIRS, GROUP, 2 * GROUP), F32),
            pltpu.VMEM((4, 256, ROWS), BF16),
            pltpu.VMEM((2, 256, ROWS), BF16),
            pltpu.VMEM((4, 256, ROWS), BF16),
            pltpu.VMEM((2, 256, ROWS), BF16),
            pltpu.VMEM((ROWS, D), BF16),
            pltpu.VMEM((ROWS, 3 * D), BF16),
            pltpu.VMEM((ROWS, 3 * D), BF16),
            pltpu.VMEM((STREAMS, 64, 16, 128), BF16),
            pltpu.VMEM((STREAMS, 64, 16, 128), BF16),
            pltpu.VMEM((ROWS, D), BF16),
            pltpu.VMEM(blocks, BF16),
            pltpu.VMEM((ROWS, D), F32),
            pltpu.SemaphoreType.DMA((5,)),
            pltpu.SemaphoreType.DMA((3, FRAMES)),
            pltpu.SemaphoreType.DMA((3, FRAMES)),
            pltpu.SemaphoreType.DMA((17,)),
            pltpu.SemaphoreType.DMA((17,)),
            pltpu.SemaphoreType.DMA((STREAMS, 3)),
            pltpu.SemaphoreType.DMA((STREAMS, 3)),
        ],
        compiler_params=pltpu.CompilerParams(
            collective_id=0, has_side_effects=True, vmem_limit_bytes=60 * 1024 * 1024
        ),
        cost_estimate=pl.CostEstimate(flops=12 * 10**9, bytes_accessed=12 * 2**20, transcendentals=2**20),
    )(clips.reshape(blocks), w_qkv, w_out, cotangent.reshape(blocks))

    def finish(*refs):
        copies = [pltpu.make_async_copy(refs[i], refs[3 + i], refs[6].at[i]) for i in range(3)]
        for copy in copies:
            copy.start()
        for copy in copies:
            copy.wait()

    out, grad_qkv, grad_out = pl.pallas_call(
        finish,
        out_shape=tuple(jax.ShapeDtypeStruct(a.shape, a.dtype) for a in (out, grad_qkv, grad_out)),
        in_specs=[vmem] * 3,
        out_specs=(any_,) * 3,
        scratch_shapes=[pltpu.SemaphoreType.DMA((3,))],
    )(out, grad_qkv, grad_out)
    return out.reshape(clips.shape), grad_qkv, grad_out


def solution(mesh):
    return jax.shard_map(
        shards,
        mesh=mesh,
        in_specs=(P("clip", "tm", None, None), P(), P(), P("clip", "tm", None, None)),
        out_specs=(P("clip", "tm", None, None), P(("clip", "tm"), None), P(("clip", "tm"), None)),
        check_vma=False,
    )
```
